768 devices in a mesh: row: 96 (over z, x, y_hi), col: 8 (over y_lo, core).
Axes of the slice: x: 4, y: 8 (y_hi: 2, y_lo: 4; y = y_hi * 4 + y_lo), z: 12, core: 2. Of those that a mesh axis runs over, the one named last changes fastest.
Arguments:
- vectors: float32 [393216, 16], P(('row', 'col')), may hold values from -6 to 6
- tiles: float32 [96, 8, 256, 64, 64], P('row', 'col'), may hold values from -0.125 to 0.125
- tile_rows: int32 [96, 8, 256], P('row', 'col'), may hold values from 0 to 63
- tile_cols: int32 [96, 8, 256], P('row', 'col'), may hold values from 0 to 767
- tile_count: int32 [96, 8], P('row', 'col'), may hold values from 1 to 256, as said below
Outputs:
- product: float32 [393216, 16], P(('row', 'col'))
The draws below stay inside these ranges and needn't reach their ends.
Inputs may be any that keep to these rules, and one draw needn't show every extreme that they name: `tile_count`: device (0, c) has all 256 slots live; devices further along row hold fewer.
All inputs are finite; a program needn't handle non-finite values.
Results may differ from the reference program's by a relative error of at most 0.0001.
Values sent between devices are 32-bit elements; how exact they have to be, the bound alone decides.
No kernel may reach another device: no remote copies, remote signals or barrier semaphores. Data moves between devices by JAX's collectives and lax.ppermute only.
A program may use at most 64 MiB of HBM per device.

```python
import jax
import jax.numpy as jnp
from jax import lax

VEC = 16
TILE = 64
TPD = 256
S = 512
RT = 64
CT = 768
M = 393216
N_ROW = 96
N_COL = 8


def draw_tile_count(key, part):
    key = jax.random.fold_in(key, 7)
    rowid = jnp.arange(N_ROW, dtype=jnp.int32)[:, None] + jnp.zeros((N_ROW, N_COL), jnp.int32)
    base = TPD - (TPD - 1) * rowid // N_ROW
    jitter = jax.random.randint(key, (N_ROW, N_COL), 0, TPD // 4 + 1) * (rowid > 0).astype(jnp.int32)
    return jnp.maximum(base - jitter, 1).astype(jnp.int32)


def with_ends(drawn, rng, least, top_value):
    index_at = [jax.random.randint(jax.random.fold_in(rng, axis), (), 0, length) for axis, length in enumerate(drawn.shape)]
    main_axis = drawn.shape.index(max(drawn.shape))
    next_to = index_at[:main_axis] + [(index_at[main_axis] + 1) % drawn.shape[main_axis]] + index_at[main_axis + 1:]
    return drawn.at[tuple(index_at)].set(least).at[tuple(next_to)].set(top_value)


def steps_of(rng, dims, shards, smallest, top_value):
    gain = 1.0
    for dim, shards_of in shards:
        draws = jax.random.uniform(jax.random.fold_in(jax.random.fold_in(rng, 6), dim), (shards_of,), jnp.float32, smallest / len(shards), top_value / len(shards))
        gain = gain * jnp.repeat(jnp.exp(draws), dims[dim] // shards_of).reshape((-1,) + (1,) * (len(dims) - 1 - dim))
    return gain


def scatter_about(stream_key, dims, scale, bound, pieces=(), held_as=jnp.bfloat16):
    loudness = steps_of(stream_key, dims, pieces, -0.22, 0.18) if pieces else 1.0
    entries = jax.random.normal(stream_key, dims, jnp.float32) * scale * loudness
    return jnp.minimum(jnp.maximum(entries, -bound), bound).astype(held_as)


def setup_inputs(seed: int = 0) -> dict:
    keys = jax.random.split(jax.random.key(seed), 6)
    vectors = scatter_about(keys[0], (M, VEC), 1.0, 6.0, ((0, 768),), jnp.float32)
    tiles = scatter_about(keys[1], (N_ROW, N_COL, TPD, TILE, TILE), (TILE * TPD * N_COL // RT) ** -0.5, 0.125, ((0, 96), (1, 8)), jnp.float32)
    tile_rows = with_ends(jax.random.randint(keys[2], (N_ROW, N_COL, TPD), 0, RT), jax.random.fold_in(keys[2], 1), 0, RT - 1).astype(jnp.int32)
    tile_cols = with_ends(jax.random.randint(keys[3], (N_ROW, N_COL, TPD), 0, CT), jax.random.fold_in(keys[3], 1), 0, CT - 1).astype(jnp.int32)
    tile_count = draw_tile_count(jax.random.fold_in(keys[5], 71), 0)
    return {"vectors": vectors, "tiles": tiles, "tile_rows": tile_rows, "tile_cols": tile_cols, "tile_count": tile_count}


def reference(vectors, tiles, tile_rows, tile_cols, tile_count):
    width = vectors.shape[1]
    grid = vectors.reshape(N_ROW, N_COL, S, width)
    total = jnp.zeros((N_ROW, N_COL, S, width), jnp.float32)

    def cell(index, total):
        rowid = (index // N_COL).astype(jnp.int32)
        colid = (index % N_COL).astype(jnp.int32)
        row_side = lax.dynamic_index_in_dim(grid, rowid, 0, False).reshape(RT, TILE, width)
        col_side = lax.dynamic_index_in_dim(grid, colid, 1, False).reshape(CT, TILE, width)
        block = tiles[rowid, colid]
        rids = tile_rows[rowid, colid]
        cids = tile_cols[rowid, colid]
        live = (jnp.arange(TPD) < tile_count[rowid, colid]).astype(jnp.float32)[:, None, None]
        forward = jnp.einsum('tab,tbv->tav', block, col_side[cids], precision=lax.Precision.HIGHEST) * live
        backward = jnp.einsum('tab,tav->tbv', block, row_side[rids], precision=lax.Precision.HIGHEST) * live
        row_part = jax.ops.segment_sum(forward, rids, num_segments=RT).reshape(N_COL, S, width)
        col_part = jax.ops.segment_sum(backward, cids, num_segments=CT).reshape(N_ROW, S, width)
        total = total.at[rowid].add(row_part)
        total = total.at[:, colid].add(col_part)
        return total

    total = lax.fori_loop(0, N_ROW * N_COL, cell, total)
    return total.reshape(M, width)
```

```python
import jax
import jax.numpy as jnp
from jax import lax
from jax.experimental import pallas as pl
from jax.experimental.pallas import tpu as pltpu
from jax.sharding import PartitionSpec as P

VEC = 16
TILE = 64
TPD = 256
S = 512
RT = 64
CT = 768
NZ, NX, NY = 12, 4, 2
PT = S // TILE
WIDE = VEC * TILE
CHUNK = CT // NX
GROUP = 4
LANES = 128
NT = (((1,), (1,)), ((), ()))


def row_index(z, x, y):
    return ((z % NZ) * NX + (x % NX)) * NY + (y % NY)


def row_shift(dx=0, dy=0):
    return [
        (row_index(z, x, y), row_index(z, x + dx, y + dy))
        for z in range(NZ)
        for x in range(NX)
        for y in range(NY)
    ]


Z_GROUPS = [[row_index(z, x, y) for z in range(NZ)] for x in range(NX) for y in range(NY)]
XY_GROUPS = [[row_index(z, x, y) for x in range(NX) for y in range(NY)] for z in range(NZ)]


def three_parts(value):
    first = value.astype(jnp.bfloat16)
    rest = value - first.astype(jnp.float32)
    second = rest.astype(jnp.bfloat16)
    third = (rest - second.astype(jnp.float32)).astype(jnp.bfloat16)
    return first, second, third


def select(onehot, value, dims=(((1,), (0,)), ((), ()))):
    parts = [
        lax.dot_general(onehot, part, dims, preferred_element_type=jnp.float32)
        for part in three_parts(value)
    ]
    return (parts[2] + parts[1]) + parts[0]


def indicator(condition):
    return jnp.where(condition, 1.0, 0.0).astype(jnp.bfloat16)


def iota(shape, dim):
    return lax.broadcasted_iota(jnp.int32, shape, dim)


def put(halves, value):
    for half in range(TPD // LANES):
        halves[half] = value[:, half * LANES : (half + 1) * LANES]


def whole(halves):
    return jnp.concatenate([halves[half] for half in range(TPD // LANES)], axis=1)


def backward_kernel(count, rids_down, cids_across, row_side, tiles, out, picked, summed):
    at_row = indicator(iota((TPD, RT), 1) == rids_down[...])
    put(picked, select(at_row, row_side[...]).T)
    live = iota((1, TPD), 1) < count[0, 0]
    at_col = indicator((iota((CT, TPD), 0) == cids_across[...]) & live)
    for group in range(VEC // GROUP):
        for half in range(TPD // LANES):
            lanes = pl.ds(half * LANES, LANES)

            def step(a, totals):
                tile = tiles[a, :, lanes]
                return tuple(
                    total + tile * picked[half, pl.ds((group * GROUP + v) * TILE + a, 1), :]
                    for v, total in enumerate(totals)
                )

            zero = jnp.zeros((TILE, LANES), jnp.float32)
            totals = lax.fori_loop(0, TILE, step, (zero,) * GROUP, unroll=4)
            for v, total in enumerate(totals):
                summed[half, v * TILE : (v + 1) * TILE, :] = total
        out[:, group * GROUP * TILE : (group + 1) * GROUP * TILE] = select(at_col, whole(summed), NT)


def forward_kernel(count, rids_across, places_down, *refs):
    chunks, (tiles, out, picked, summed) = refs[:NX], refs[NX:]
    found = None
    for d, chunk in enumerate(chunks):
        at_place = indicator(iota((TPD, CHUNK), 1) + d * CHUNK == places_down[...])
        part = select(at_place, chunk[...])
        found = part if found is None else found + part
    put(picked, found.T)
    live = iota((1, TPD), 1) < count[0, 0]
    at_row = indicator((iota((RT, TPD), 0) == rids_across[...]) & live)
    for group in range(VEC // GROUP):
        for half in range(TPD // LANES):
            lanes = pl.ds(half * LANES, LANES)
            blocks = [
                picked[half, (group * GROUP + v) * TILE : (group * GROUP + v + 1) * TILE, :]
                for v in range(GROUP)
            ]

            def step(a, carry):
                tile = tiles[a, :, lanes]
                for v, block in enumerate(blocks):
                    summed[half, pl.ds(v * TILE + a, 1), :] = jnp.sum(
                        tile * block, axis=0, keepdims=True
                    )
                return carry

            lax.fori_loop(0, TILE, step, 0, unroll=4)
        out[:, group * GROUP * TILE : (group + 1) * GROUP * TILE] = select(at_row, whole(summed), NT)


def run(kernel, rows, count, *operands):
    in_vmem = pl.BlockSpec(memory_space=pltpu.VMEM)
    return pl.pallas_call(
        kernel,
        out_shape=jax.ShapeDtypeStruct((rows, WIDE), jnp.float32),
        in_specs=[pl.BlockSpec(memory_space=pltpu.SMEM)] + [in_vmem] * len(operands),
        out_specs=in_vmem,
        scratch_shapes=[
            pltpu.VMEM((TPD // LANES, WIDE, LANES), jnp.float32),
            pltpu.VMEM((TPD // LANES, GROUP * TILE, LANES), jnp.float32),
        ],
        compiler_params=pltpu.CompilerParams(vmem_limit_bytes=40 * 1024 * 1024),
        cost_estimate=pl.CostEstimate(
            flops=2 * TPD * TILE * TILE * VEC, bytes_accessed=8 * 1024 * 1024, transcendentals=0
        ),
    )(count, *operands)


def local(vectors, tiles, tile_rows, tile_cols, tile_count):
    me = lax.axis_index("row")
    my_x, my_y = (me >> 1) & 3, me & 1
    piece = vectors.T.reshape(VEC, PT, TILE).transpose(1, 0, 2).reshape(PT, WIDE)
    block = tiles[0, 0].transpose(1, 2, 0)
    rids, cids = tile_rows[0], tile_cols[0]

    other = lax.ppermute(piece, "row", row_shift(dy=1))
    row_side = lax.all_gather(piece, "col", axis=0, tiled=True)
    col_part = run(backward_kernel, CT, tile_count, rids.T, cids, row_side, block)
    col_sum = lax.psum_scatter(
        col_part, "row", axis_index_groups=Z_GROUPS, scatter_dimension=0, tiled=True
    )

    mine = lax.all_gather(
        jnp.concatenate([piece, other]), "row", axis_index_groups=Z_GROUPS, axis=0, tiled=True
    )
    chunks = [mine] + [lax.ppermute(mine, "row", row_shift(dx=d)) for d in range(1, NX)]
    z, x, y, rest = cids >> 6, (cids >> 4) & 3, (cids >> 3) & 1, cids & 7
    places = ((my_x - x) & 3) * CHUNK + (z * NY + (y ^ my_y)) * PT + rest
    row_part = run(forward_kernel, RT, tile_count, rids, places.T, *chunks, block)

    col_terms = lax.all_to_all(
        col_sum, "row", 0, 0, axis_index_groups=XY_GROUPS, tiled=True
    ).reshape(NX * NY, PT, WIDE)
    row_terms = lax.all_to_all(row_part, "col", 0, 0, tiled=True).reshape(-1, PT, WIDE)
    total = col_terms.sum(axis=0) + row_terms.sum(axis=0)
    return total.reshape(PT, VEC, TILE).transpose(1, 0, 2).reshape(VEC, S).T


def solution(mesh):
    placed = (
        P(("row", "col"), None),
        P("row", "col", None, None, None),
        P("row", "col", None),
        P("row", "col", None),
        P("row", "col"),
    )
    return jax.shard_map(
        local, mesh=mesh, in_specs=placed, out_specs=P(("row", "col"), None), check_vma=False
    )
```

```python
import jax
import jax.numpy as jnp
from jax import lax
from jax.experimental import pallas as pl
from jax.experimental.pallas import tpu as pltpu
from jax.sharding import PartitionSpec as P

VEC = 16
TILE = 64
TPD = 256
S = 512
RT = 64
CT = 768
NZ, NX, NY = 12, 4, 2
NCOL = 8
PT = S // TILE
WIDE = VEC * TILE
CHUNK = CT // NX
GROUP = 4
LANES = 128
NT = (((1,), (1,)), ((), ()))


def row_index(z, x, y):
    return ((z % NZ) * NX + (x % NX)) * NY + (y % NY)


def row_shift(dx=0, dy=0):
    return [
        (row_index(z, x, y), row_index(z, x + dx, y + dy))
        for z in range(NZ)
        for x in range(NX)
        for y in range(NY)
    ]


Z_GROUPS = [[row_index(z, x, y) for z in range(NZ)] for x in range(NX) for y in range(NY)]
RING_GROUPS = [
    [row_index(z, x, y) * NCOL + c for y in range(NY) for c in range(NCOL)]
    for z in range(NZ)
    for x in range(NX)
]
XY_GROUPS = [[row_index(z, x, y) for x in range(NX) for y in range(NY)] for z in range(NZ)]


def three_parts(value):
    first = value.astype(jnp.bfloat16)
    rest = value - first.astype(jnp.float32)
    second = rest.astype(jnp.bfloat16)
    third = (rest - second.astype(jnp.float32)).astype(jnp.bfloat16)
    return first, second, third


def select(onehot, value, dims=(((1,), (0,)), ((), ()))):
    return lax.dot_general(
        jnp.concatenate([onehot] * 3, axis=dims[0][0][0]),
        jnp.concatenate(three_parts(value), axis=dims[0][1][0]),
        dims,
        preferred_element_type=jnp.float32,
    )


def indicator(condition):
    return jnp.where(condition, 1.0, 0.0).astype(jnp.bfloat16)


def iota(shape, dim):
    return lax.broadcasted_iota(jnp.int32, shape, dim)


def put(halves, value):
    for half in range(TPD // LANES):
        halves[half] = value[:, half * LANES : (half + 1) * LANES]


def whole(halves):
    return jnp.concatenate([halves[half] for half in range(TPD // LANES)], axis=1)


def column(row):
    return jnp.broadcast_to(row, (8, row.shape[1])).T[:, :1]


def fetch(pairs, arrived):
    copies = [pltpu.make_async_copy(*pair, arrived.at[i]) for i, pair in enumerate(pairs)]
    for copy in copies:
        copy.start()
    return copies


def backward_kernel(count, row_side, rids_far, cids_far, far, out, tiles, rids, cids, arrived, picked, summed):
    copies = fetch([(rids_far, rids), (cids_far, cids), (far, tiles)], arrived)
    copies[0].wait()
    copies[1].wait()
    at_row = indicator(iota((NY * RT, TPD), 0) == rids[...])
    put(picked, lax.dot_general(jnp.concatenate(three_parts(row_side[...])), jnp.concatenate([at_row] * 3), (((0,), (0,)), ((), ())), preferred_element_type=jnp.float32))
    live = iota((1, TPD), 1) < count[0, 0]
    at_col = indicator((iota((CT, TPD), 0) == cids[...]) & live)
    copies[2].wait()
    for group in range(VEC // GROUP):
        for half in range(TPD // LANES):
            lanes = pl.ds(half * LANES, LANES)

            def step(a, totals):
                tile = tiles[a, :, lanes]
                return tuple(
                    total + tile * picked[half, pl.ds((group * GROUP + v) * TILE + a, 1), :]
                    for v, total in enumerate(totals)
                )

            zero = jnp.zeros((TILE, LANES), jnp.float32)
            totals = lax.fori_loop(0, TILE, step, (zero,) * GROUP, unroll=16)
            for v, total in enumerate(totals):
                summed[half, v * TILE : (v + 1) * TILE, :] = total
        out[:, group * GROUP * TILE : (group + 1) * GROUP * TILE] = select(at_col, whole(summed), NT)


def forward_kernel(count, places, *refs):
    chunks, (rids_far, far, out, tiles, rids, _, arrived, picked, summed) = refs[:-9], refs[-9:]
    copies = fetch([(rids_far, rids), (far, tiles)], arrived)
    at_place = indicator(iota((CT, TPD), 0) == places[...])
    put(picked, lax.dot_general(jnp.concatenate(three_parts(jnp.concatenate([chunk[...] for chunk in chunks]))), jnp.concatenate([at_place] * 3), (((0,), (0,)), ((), ())), preferred_element_type=jnp.float32))
    copies[0].wait()
    live = iota((1, TPD), 1) < count[0, 0]
    at_row = indicator((iota((RT, TPD), 0) == rids[...]) & live)
    copies[1].wait()
    for group in range(VEC // GROUP):
        for half in range(TPD // LANES):
            lanes = pl.ds(half * LANES, LANES)
            blocks = [
                picked[half, (group * GROUP + v) * TILE : (group * GROUP + v + 1) * TILE, :]
                for v in range(GROUP)
            ]

            def step(a, carry):
                tile = tiles[a, :, lanes]
                for v, block in enumerate(blocks):
                    summed[half, pl.ds(v * TILE + a, 1), :] = jnp.sum(
                        tile * block, axis=0, keepdims=True
                    )
                return carry

            lax.fori_loop(0, TILE, step, 0, unroll=16)
        out[:, group * GROUP * TILE : (group + 1) * GROUP * TILE] = select(at_row, whole(summed), NT)


def run(kernel, rows, far, count, *operands):
    in_vmem = pl.BlockSpec(memory_space=pltpu.VMEM)
    return pl.pallas_call(
        kernel,
        out_shape=jax.ShapeDtypeStruct((rows, WIDE), jnp.float32),
        in_specs=[pl.BlockSpec(memory_space=pltpu.SMEM)]
        + [in_vmem] * (len(operands) - far)
        + [pl.BlockSpec(memory_space=pltpu.HBM)] * far,
        out_specs=in_vmem,
        scratch_shapes=[
            pltpu.VMEM((TILE, TILE, TPD), jnp.float32),
            pltpu.VMEM((1, TPD), jnp.int32),
            pltpu.VMEM((1, TPD), jnp.int32),
            pltpu.SemaphoreType.DMA((3,)),
            pltpu.VMEM((TPD // LANES, WIDE, LANES), jnp.float32),
            pltpu.VMEM((TPD // LANES, GROUP * TILE, LANES), jnp.float32),
        ],
        compiler_params=pltpu.CompilerParams(vmem_limit_bytes=58 * 1024 * 1024),
        cost_estimate=pl.CostEstimate(
            flops=10_000_000_000, bytes_accessed=8 * 1024 * 1024, transcendentals=0
        ),
    )(count, *operands)


def local(vectors, tiles, tile_rows, tile_cols, tile_count):
    me, me_col = lax.axis_index("row"), lax.axis_index("col")
    my_x, my_y = (me >> 1) & 3, me & 1
    piece = vectors.T.reshape(VEC, PT, TILE).transpose(1, 0, 2).reshape(PT, WIDE)
    block = tiles[0, 0].transpose(1, 2, 0)
    rids, cids = tile_rows[0], tile_cols[0]

    rows = lax.all_gather(
        piece, ("row", "col"), axis_index_groups=RING_GROUPS, axis=0, tiled=True
    )
    my_rids = rids + my_y * RT
    col_part = run(backward_kernel, CT, 3, tile_count, rows, my_rids, cids, block)
    col_sum = lax.psum_scatter(
        col_part, "row", axis_index_groups=Z_GROUPS, scatter_dimension=0, tiled=True
    )

    mine = lax.all_gather(
        lax.dynamic_slice_in_dim(rows.reshape(NY, -1, WIDE), me_col * PT, PT, 1).reshape(-1, WIDE),
        "row",
        axis_index_groups=Z_GROUPS,
        axis=0,
        tiled=True,
    )
    first, second = mine[: CHUNK // 2], mine[CHUNK // 2 :]
    left_first = lax.ppermute(first, "row", row_shift(dx=1))
    right_second = lax.ppermute(second, "row", row_shift(dx=-1))
    left_second = lax.ppermute(second, "row", row_shift(dx=1))
    right_first = lax.ppermute(first, "row", row_shift(dx=-1))
    far_first = lax.ppermute(left_first, "row", row_shift(dx=1))
    far_second = lax.ppermute(right_second, "row", row_shift(dx=-1))
    chunks = [mine, left_first, left_second, far_first, far_second, right_first, right_second]
    z, x, y, rest = cids >> 6, (cids >> 4) & 3, (cids >> 3) & 1, cids & 7
    places = ((my_x - x) & 3) * CHUNK + (z * NY + y) * PT + rest
    places, col_sum = lax.optimization_barrier((places, col_sum))
    col_terms = lax.all_to_all(
        col_sum, "row", 0, 0, axis_index_groups=XY_GROUPS, tiled=True
    ).reshape(NX * NY, PT, WIDE)
    row_part = run(forward_kernel, RT, 2, tile_count, places, *chunks, rids, block)
    row_terms = lax.all_to_all(row_part, "col", 0, 0, tiled=True).reshape(-1, PT, WIDE)
    total = col_terms.sum(axis=0) + row_terms.sum(axis=0)
    return total.reshape(PT, VEC, TILE).transpose(1, 0, 2).reshape(VEC, S).T


def solution(mesh):
    placed = (
        P(("row", "col"), None),
        P("row", "col", None, None, None),
        P("row", "col", None),
        P("row", "col", None),
        P("row", "col"),
    )
    return jax.shard_map(
        local, mesh=mesh, in_specs=placed, out_specs=P(("row", "col"), None), check_vma=False
    )
```

```python
import jax
import jax.numpy as jnp
from jax import lax
from jax.experimental import pallas as pl
from jax.experimental.pallas import tpu as pltpu
from jax.sharding import PartitionSpec as P

VEC = 16
TILE = 64
TPD = 256
S = 512
RT = 64
CT = 768
NZ, NX, NY = 12, 4, 2
NCOL = 8
PT = S // TILE
WIDE = VEC * TILE
CHUNK = CT // NX
GROUP = 4
LANES = 128
CHUNKS = 7
VMEM_LIMIT = 58 * 1024 * 1024


def row_index(z, x, y):
    return ((z % NZ) * NX + (x % NX)) * NY + (y % NY)


def row_shift(dx=0, dy=0):
    return [
        (row_index(z, x, y), row_index(z, x + dx, y + dy))
        for z in range(NZ)
        for x in range(NX)
        for y in range(NY)
    ]


Z_GROUPS = [[row_index(z, x, y) for z in range(NZ)] for x in range(NX) for y in range(NY)]
RING_GROUPS = [
    [row_index(z, x, y) * NCOL + c for y in range(NY) for c in range(NCOL)]
    for z in range(NZ)
    for x in range(NX)
]
XY_GROUPS = [[row_index(z, x, y) for x in range(NX) for y in range(NY)] for z in range(NZ)]


def three_parts(value):
    first = value.astype(jnp.bfloat16)
    rest = value - first.astype(jnp.float32)
    second = rest.astype(jnp.bfloat16)
    third = (rest - second.astype(jnp.float32)).astype(jnp.bfloat16)
    return first, second, third


def indicator(condition):
    return jnp.where(condition, 1.0, 0.0).astype(jnp.bfloat16)


def iota(shape, dim):
    return lax.broadcasted_iota(jnp.int32, shape, dim)


def put(halves, value):
    for half in range(TPD // LANES):
        halves[half] = value[:, half * LANES : (half + 1) * LANES]


def whole(halves):
    return jnp.concatenate([halves[half] for half in range(TPD // LANES)], axis=1)


def column(row):
    return jnp.broadcast_to(row, (8, row.shape[1])).T[:, :1]


def fetch(pairs, arrived):
    copies = [pltpu.make_async_copy(*pair, arrived.at[i]) for i, pair in enumerate(pairs)]
    for copy in copies:
        copy.start()
    return copies


def pick(picked, onehot, value):
    dims = (((0,), (0,)), ((), ()))
    put(
        picked,
        lax.dot_general(
            jnp.concatenate(three_parts(value)),
            jnp.concatenate([onehot] * 3),
            dims,
            preferred_element_type=jnp.float32,
        ),
    )


def place(onehot, value):
    return lax.dot_general(
        jnp.concatenate([onehot] * 3, axis=1),
        jnp.concatenate(three_parts(value), axis=1),
        (((1,), (1,)), ((), ())),
        preferred_element_type=jnp.float32,
    )


def backward_kernel(count, base, rows, rids_far, cids_far, far, out, side, rids, cids, tiles, arrived, picked, summed):
    own = rows.at[pl.ds(pl.multiple_of(base[0, 0], RT), RT)]
    copies = fetch([(own, side), (rids_far, rids), (cids_far, cids), (far, tiles)], arrived)
    for copy in copies[:3]:
        copy.wait()
    pick(picked, indicator(iota((RT, TPD), 0) == rids[...]), side[...])
    live = iota((1, TPD), 1) < count[0, 0]
    at_col = indicator((iota((CT, TPD), 0) == cids[...]) & live)
    copies[3].wait()
    for group in range(VEC // GROUP):
        for half in range(TPD // LANES):
            lanes = pl.ds(half * LANES, LANES)

            def step(a, totals):
                tile = tiles[a, :, lanes]
                return tuple(
                    total + tile * picked[half, pl.ds((group * GROUP + v) * TILE + a, 1), :]
                    for v, total in enumerate(totals)
                )

            zero = jnp.zeros((TILE, LANES), jnp.float32)
            totals = lax.fori_loop(0, TILE, step, (zero,) * GROUP, unroll=64)
            for v, total in enumerate(totals):
                summed[half, v * TILE : (v + 1) * TILE, :] = total
        out[:, group * GROUP * TILE : (group + 1) * GROUP * TILE] = place(at_col, whole(summed))


def forward_kernel(count, *refs):
    chunks, refs = refs[:CHUNKS], refs[CHUNKS:]
    places_far, rids_far, far, out, side, rids, places, tiles, arrived, picked, summed = refs
    pairs = [(places_far, places), (rids_far, rids)]
    start = 0
    for chunk in chunks:
        pairs.append((chunk, side.at[pl.ds(start, chunk.shape[0])]))
        start += chunk.shape[0]
    copies = fetch(pairs + [(far, tiles)], arrived)
    for copy in copies[:-1]:
        copy.wait()
    pick(picked, indicator(iota((CT, TPD), 0) == places[...]), side[...])
    live = iota((1, TPD), 1) < count[0, 0]
    at_row = indicator((iota((RT, TPD), 0) == rids[...]) & live)
    copies[-1].wait()
    for group in range(VEC // GROUP):
        for half in range(TPD // LANES):
            lanes = pl.ds(half * LANES, LANES)
            blocks = [
                picked[half, (group * GROUP + v) * TILE : (group * GROUP + v + 1) * TILE, :]
                for v in range(GROUP)
            ]

            def step(a, carry):
                tile = tiles[a, :, lanes]
                for v, block in enumerate(blocks):
                    summed[half, pl.ds(v * TILE + a, 1), :] = jnp.sum(
                        tile * block, axis=0, keepdims=True
                    )
                return carry

            lax.fori_loop(0, TILE, step, 0, unroll=64)
        out[:, group * GROUP * TILE : (group + 1) * GROUP * TILE] = place(at_row, whole(summed))


def run(kernel, rows, side, scalars, *operands):
    return pl.pallas_call(
        kernel,
        out_shape=jax.ShapeDtypeStruct((rows, WIDE), jnp.float32),
        in_specs=[pl.BlockSpec(memory_space=pltpu.SMEM)] * len(scalars)
        + [pl.BlockSpec(memory_space=pltpu.HBM)] * len(operands),
        out_specs=pl.BlockSpec(memory_space=pltpu.VMEM),
        scratch_shapes=[
            pltpu.VMEM((side, WIDE), jnp.float32),
            pltpu.VMEM((1, TPD), jnp.int32),
            pltpu.VMEM((1, TPD), jnp.int32),
            pltpu.VMEM((TILE, TILE, TPD), jnp.float32),
            pltpu.SemaphoreType.DMA((len(operands),)),
            pltpu.VMEM((TPD // LANES, WIDE, LANES), jnp.float32),
            pltpu.VMEM((TPD // LANES, GROUP * TILE, LANES), jnp.float32),
        ],
        compiler_params=pltpu.CompilerParams(vmem_limit_bytes=VMEM_LIMIT),
        cost_estimate=pl.CostEstimate(
            flops=10_000_000_000, bytes_accessed=8 * 1024 * 1024, transcendentals=0
        ),
    )(*scalars, *operands)


def local(vectors, tiles, tile_rows, tile_cols, tile_count):
    me, me_col = lax.axis_index("row"), lax.axis_index("col")
    my_x, my_y = (me >> 1) & 3, me & 1
    piece = vectors.T.reshape(VEC, PT, TILE).transpose(1, 0, 2).reshape(PT, WIDE)
    block = tiles[0, 0].transpose(1, 2, 0)
    rids, cids = tile_rows[0], tile_cols[0]

    rows = lax.all_gather(
        piece, ("row", "col"), axis_index_groups=RING_GROUPS, axis=0, tiled=True
    )
    base = (my_y * RT).reshape(1, 1)
    col_part = run(backward_kernel, CT, RT, (tile_count, base), rows, rids, cids, block)
    col_sum = lax.psum_scatter(
        col_part, "row", axis_index_groups=Z_GROUPS, scatter_dimension=0, tiled=True
    )

    mine = lax.all_gather(
        lax.dynamic_slice_in_dim(rows.reshape(NY, -1, WIDE), me_col * PT, PT, 1).reshape(-1, WIDE),
        "row",
        axis_index_groups=Z_GROUPS,
        axis=0,
        tiled=True,
    )
    first, second = mine[: CHUNK // 2], mine[CHUNK // 2 :]
    left_first = lax.ppermute(first, "row", row_shift(dx=1))
    right_second = lax.ppermute(second, "row", row_shift(dx=-1))
    left_second = lax.ppermute(second, "row", row_shift(dx=1))
    right_first = lax.ppermute(first, "row", row_shift(dx=-1))
    far_first = lax.ppermute(left_first, "row", row_shift(dx=1))
    far_second = lax.ppermute(right_second, "row", row_shift(dx=-1))
    chunks = [mine, left_first, left_second, far_first, far_second, right_first, right_second]
    z, x, y, rest = cids >> 6, (cids >> 4) & 3, (cids >> 3) & 1, cids & 7
    places = ((my_x - x) & 3) * CHUNK + (z * NY + y) * PT + rest
    places, col_sum = lax.optimization_barrier((places, col_sum))
    col_terms = lax.all_to_all(
        col_sum, "row", 0, 0, axis_index_groups=XY_GROUPS, tiled=True
    ).reshape(NX * NY, PT, WIDE)
    row_part = run(forward_kernel, RT, CT, (tile_count,), *chunks, places, rids, block)
    row_terms = lax.all_to_all(row_part, "col", 0, 0, tiled=True).reshape(-1, PT, WIDE)
    total = col_terms.sum(axis=0) + row_terms.sum(axis=0)
    return total.reshape(PT, VEC, TILE).transpose(1, 0, 2).reshape(VEC, S).T


def solution(mesh):
    placed = (
        P(("row", "col"), None),
        P("row", "col", None, None, None),
        P("row", "col", None),
        P("row", "col", None),
        P("row", "col"),
    )
    return jax.shard_map(
        local, mesh=mesh, in_specs=placed, out_specs=P(("row", "col"), None), check_vma=False
    )
```

```python
import jax
import jax.numpy as jnp
from jax import lax
from jax.experimental import pallas as pl
from jax.experimental.pallas import tpu as pltpu
from jax.sharding import PartitionSpec as P

VEC = 16
TILE = 64
TPD = 256
S = 512
RT = 64
CT = 768
NZ, NX, NY = 12, 4, 2
NCOL, NYL = 8, 4
PT = S // TILE
WIDE = VEC * TILE
CHUNK = CT // NX
GROUP = 4
LANES = 128
CHUNKS = 7
VMEM_LIMIT = 58 * 1024 * 1024


def row_index(z, x, y):
    return ((z % NZ) * NX + (x % NX)) * NY + (y % NY)


def col_shift(dy=0, core=0):
    return [
        (y * 2 + k, ((y + dy) % NYL) * 2 + (k ^ core)) for y in range(NYL) for k in range(2)
    ]


def row_shift(dx=0, dy=0):
    return [
        (row_index(z, x, y), row_index(z, x + dx, y + dy))
        for z in range(NZ)
        for x in range(NX)
        for y in range(NY)
    ]


Z_GROUPS = [[row_index(z, x, y) for z in range(NZ)] for x in range(NX) for y in range(NY)]
RING_GROUPS = [
    [row_index(z, x, y) * NCOL + c for y in range(NY) for c in range(NCOL)]
    for z in range(NZ)
    for x in range(NX)
]
XY_GROUPS = [[row_index(z, x, y) for x in range(NX) for y in range(NY)] for z in range(NZ)]


def three_parts(value):
    first = value.astype(jnp.bfloat16)
    rest = value - first.astype(jnp.float32)
    second = rest.astype(jnp.bfloat16)
    third = (rest - second.astype(jnp.float32)).astype(jnp.bfloat16)
    return first, second, third


def indicator(condition):
    return jnp.where(condition, 1.0, 0.0).astype(jnp.bfloat16)


def iota(shape, dim):
    return lax.broadcasted_iota(jnp.int32, shape, dim)


def put(halves, value):
    for half in range(TPD // LANES):
        halves[half] = value[:, half * LANES : (half + 1) * LANES]


def whole(halves):
    return jnp.concatenate([halves[half] for half in range(TPD // LANES)], axis=1)


def column(row):
    return jnp.broadcast_to(row, (8, row.shape[1])).T[:, :1]


def fetch(pairs, arrived):
    copies = [pltpu.make_async_copy(*pair, arrived.at[i]) for i, pair in enumerate(pairs)]
    for copy in copies:
        copy.start()
    return copies


def pick(picked, onehot, value):
    dims = (((0,), (0,)), ((), ()))
    put(
        picked,
        lax.dot_general(
            jnp.concatenate(three_parts(value)),
            jnp.concatenate([onehot] * 3),
            dims,
            preferred_element_type=jnp.float32,
        ),
    )


def place(onehot, value):
    return lax.dot_general(
        jnp.concatenate([onehot] * 3, axis=1),
        jnp.concatenate(three_parts(value), axis=1),
        (((1,), (1,)), ((), ())),
        preferred_element_type=jnp.float32,
    )


def backward_kernel(count, base, rows, rids_far, cids_far, far, out, side, rids, cids, tiles, arrived, picked, summed):
    own = rows.at[pl.ds(pl.multiple_of(base[0, 0], RT), RT)]
    copies = fetch([(own, side), (rids_far, rids), (cids_far, cids), (far, tiles)], arrived)
    for copy in copies[:3]:
        copy.wait()
    pick(picked, indicator(iota((RT, TPD), 0) == rids[...]), side[...])
    live = iota((1, TPD), 1) < count[0, 0]
    at_col = indicator((iota((CT, TPD), 0) == cids[...]) & live)
    copies[3].wait()
    for group in range(VEC // GROUP):
        for half in range(TPD // LANES):
            lanes = pl.ds(half * LANES, LANES)

            def step(a, totals):
                tile = tiles[a, :, lanes]
                return tuple(
                    total + tile * picked[half, pl.ds((group * GROUP + v) * TILE + a, 1), :]
                    for v, total in enumerate(totals)
                )

            zero = jnp.zeros((TILE, LANES), jnp.float32)
            totals = lax.fori_loop(0, TILE, step, (zero,) * GROUP, unroll=64)
            for v, total in enumerate(totals):
                summed[half, v * TILE : (v + 1) * TILE, :] = total
        out[:, group * GROUP * TILE : (group + 1) * GROUP * TILE] = place(at_col, whole(summed))


def forward_kernel(count, row, col, *refs):
    chunks, refs = refs[:CHUNKS], refs[CHUNKS:]
    cids_far, rids_far, far, own, mate, side, rids, cids, tiles, arrived, picked, summed = refs
    pairs = [(cids_far, cids), (rids_far, rids)]
    start = 0
    for chunk in chunks:
        pairs.append((chunk, side.at[pl.ds(start, chunk.shape[0])]))
        start += chunk.shape[0]
    copies = fetch(pairs + [(far, tiles)], arrived)
    for copy in copies[:-1]:
        copy.wait()
    tile = cids[...]
    x, rest = (tile >> 4) & 3, (tile >> 6) * (NY * PT) + (tile & 15)
    places = (((row[0, 0] >> 1) - x) & 3) * CHUNK + rest
    pick(picked, indicator(iota((CT, TPD), 0) == places), side[...])
    tile, me = rids[...], col[0, 0]
    core, y = ((tile >> 3) ^ me) & 1, ((tile >> 4) - (me >> 1)) & 3
    places = core * (RT // 2) + y * PT + (tile & 7)
    live = iota((1, TPD), 1) < count[0, 0]
    at_row = indicator((iota((RT, TPD), 0) == places) & live)
    copies[-1].wait()
    for group in range(VEC // GROUP):
        for half in range(TPD // LANES):
            lanes = pl.ds(half * LANES, LANES)
            blocks = [
                picked[half, (group * GROUP + v) * TILE : (group * GROUP + v + 1) * TILE, :]
                for v in range(GROUP)
            ]

            def step(a, carry):
                tile = tiles[a, :, lanes]
                for v, block in enumerate(blocks):
                    summed[half, pl.ds(v * TILE + a, 1), :] = jnp.sum(
                        tile * block, axis=0, keepdims=True
                    )
                return carry

            lax.fori_loop(0, TILE, step, 0, unroll=64)
        columns = slice(group * GROUP * TILE, (group + 1) * GROUP * TILE)
        sums = place(at_row, whole(summed))
        own[:, columns], mate[:, columns] = sums[: RT // 2], sums[RT // 2 :]


def run(kernel, outs, side, scalars, *operands):
    return pl.pallas_call(
        kernel,
        out_shape=[jax.ShapeDtypeStruct((rows, WIDE), jnp.float32) for rows in outs],
        in_specs=[pl.BlockSpec(memory_space=pltpu.SMEM)] * len(scalars)
        + [pl.BlockSpec(memory_space=pltpu.HBM)] * len(operands),
        out_specs=[pl.BlockSpec(memory_space=pltpu.VMEM)] * len(outs),
        scratch_shapes=[
            pltpu.VMEM((side, WIDE), jnp.float32),
            pltpu.VMEM((1, TPD), jnp.int32),
            pltpu.VMEM((1, TPD), jnp.int32),
            pltpu.VMEM((TILE, TILE, TPD), jnp.float32),
            pltpu.SemaphoreType.DMA((len(operands),)),
            pltpu.VMEM((TPD // LANES, WIDE, LANES), jnp.float32),
            pltpu.VMEM((TPD // LANES, GROUP * TILE, LANES), jnp.float32),
        ],
        compiler_params=pltpu.CompilerParams(vmem_limit_bytes=VMEM_LIMIT),
        cost_estimate=pl.CostEstimate(
            flops=10_000_000_000, bytes_accessed=8 * 1024 * 1024, transcendentals=0
        ),
    )(*scalars, *operands)


def local(vectors, tiles, tile_rows, tile_cols, tile_count):
    me, me_col = lax.axis_index("row"), lax.axis_index("col")
    my_x, my_y = (me >> 1) & 3, me & 1
    piece = vectors.T.reshape(VEC, PT, TILE).transpose(1, 0, 2).reshape(PT, WIDE)
    block = tiles[0, 0].transpose(1, 2, 0)
    rids, cids = tile_rows[0], tile_cols[0]

    rows = lax.all_gather(
        piece, ("row", "col"), axis_index_groups=RING_GROUPS, axis=0, tiled=True
    )
    base = (my_y * RT).reshape(1, 1)
    (col_part,) = run(backward_kernel, [CT], RT, (tile_count, base), rows, rids, cids, block)
    col_sum = lax.psum_scatter(
        col_part, "row", axis_index_groups=Z_GROUPS, scatter_dimension=0, tiled=True
    )

    mine = lax.all_gather(
        lax.dynamic_slice_in_dim(rows.reshape(NY, -1, WIDE), me_col * PT, PT, 1).reshape(-1, WIDE),
        "row",
        axis_index_groups=Z_GROUPS,
        axis=0,
        tiled=True,
    )
    first, second = mine[: CHUNK // 2], mine[CHUNK // 2 :]
    left_first = lax.ppermute(first, "row", row_shift(dx=1))
    right_second = lax.ppermute(second, "row", row_shift(dx=-1))
    left_second = lax.ppermute(second, "row", row_shift(dx=1))
    right_first = lax.ppermute(first, "row", row_shift(dx=-1))
    far_first = lax.ppermute(left_first, "row", row_shift(dx=1))
    far_second = lax.ppermute(right_second, "row", row_shift(dx=-1))
    chunks = [mine, left_first, left_second, far_first, far_second, right_first, right_second]
    own, others = run(
        forward_kernel,
        [RT // 2, RT // 2],
        CT,
        (tile_count, me.reshape(1, 1), me_col.reshape(1, 1)),
        *chunks,
        cids,
        rids,
        block,
    )

    own, col_sum = lax.optimization_barrier((own, col_sum))
    col_terms = lax.all_to_all(
        col_sum, "row", 0, 0, axis_index_groups=XY_GROUPS, tiled=True
    ).reshape(NX * NY, PT, WIDE)
    mate = lax.ppermute(others, "col", col_shift(core=1))
    pair = (own + mate).reshape(NYL, PT, WIDE)
    row_total = pair[0]
    for d in range(1, NYL):
        row_total = row_total + lax.ppermute(pair[d], "col", col_shift(dy=d))
    total = col_terms.sum(axis=0) + row_total
    return total.reshape(PT, VEC, TILE).transpose(1, 0, 2).reshape(VEC, S).T


def solution(mesh):
    placed = (
        P(("row", "col"), None),
        P("row", "col", None, None, None),
        P("row", "col", None),
        P("row", "col", None),
        P("row", "col"),
    )
    return jax.shard_map(
        local, mesh=mesh, in_specs=placed, out_specs=P(("row", "col"), None), check_vma=False
    )
```

```python
import jax
import jax.numpy as jnp
from jax import lax
from jax.experimental import pallas as pl
from jax.experimental.pallas import tpu as pltpu
from jax.sharding import PartitionSpec as P

VEC = 16
TILE = 64
TPD = 256
S = 512
RT = 64
CT = 768
NZ, NX, NY = 12, 4, 2
NCOL = 8
PT = S // TILE
WIDE = VEC * TILE
CHUNK = CT // NX
GROUP = 4
LANES = 128
CHUNKS = 7
BACK_MIB, FORTH_MIB = 58, 48


def row_index(z, x, y):
    return ((z % NZ) * NX + (x % NX)) * NY + (y % NY)


def row_shift(dx=0, dy=0):
    return [
        (row_index(z, x, y), row_index(z, x + dx, y + dy))
        for z in range(NZ)
        for x in range(NX)
        for y in range(NY)
    ]


Z_GROUPS = [[row_index(z, x, y) for z in range(NZ)] for x in range(NX) for y in range(NY)]
RING_GROUPS = [
    [row_index(z, x, y) * NCOL + c for y in range(NY) for c in range(NCOL)]
    for z in range(NZ)
    for x in range(NX)
]


def three_parts(value):
    first = value.astype(jnp.bfloat16)
    rest = value - first.astype(jnp.float32)
    second = rest.astype(jnp.bfloat16)
    third = (rest - second.astype(jnp.float32)).astype(jnp.bfloat16)
    return first, second, third


def indicator(condition):
    return jnp.where(condition, 1.0, 0.0).astype(jnp.bfloat16)


def iota(shape, dim):
    return lax.broadcasted_iota(jnp.int32, shape, dim)


def put(halves, value):
    for half in range(TPD // LANES):
        halves[half] = value[:, half * LANES : (half + 1) * LANES]


def whole(halves):
    return jnp.concatenate([halves[half] for half in range(TPD // LANES)], axis=1)


def column(row):
    return jnp.broadcast_to(row, (8, row.shape[1])).T[:, :1]


def fetch(pairs, arrived):
    copies = [pltpu.make_async_copy(*pair, arrived.at[i]) for i, pair in enumerate(pairs)]
    for copy in copies:
        copy.start()
    return copies


def pick(picked, onehot, value):
    dims = (((0,), (0,)), ((), ()))
    put(
        picked,
        lax.dot_general(
            jnp.concatenate(three_parts(value)),
            jnp.concatenate([onehot] * 3),
            dims,
            preferred_element_type=jnp.float32,
        ),
    )


def place(onehot, value):
    return lax.dot_general(
        jnp.concatenate([onehot] * 3, axis=1),
        jnp.concatenate(three_parts(value), axis=1),
        (((1,), (1,)), ((), ())),
        preferred_element_type=jnp.float32,
    )


def backward_kernel(
    count, row, col, rows, rids_far, cids_far, far, out, pair, side, rids, cids, tiles, arrived, picked, summed
):
    me_x, me_y = (row[0, 0] >> 1) & 3, row[0, 0] & 1
    own = rows.at[pl.ds(pl.multiple_of(me_y * RT, RT), RT)]
    pairs = [(own, side), (rids_far, rids), (cids_far, cids), (far, tiles)]
    for y in range(NY):
        piece = rows.at[pl.ds(pl.multiple_of(y * RT + col[0, 0] * PT, PT), PT)]
        pairs.append((piece, pair.at[pl.ds(y * PT, PT)]))
    copies = fetch(pairs, arrived)
    for copy in copies[:3]:
        copy.wait()
    pick(picked, indicator(iota((RT, TPD), 0) == rids[...]), side[...])
    tile = cids[...]
    x, y = ((tile >> 4) - me_x) & 3, ((tile >> 3) ^ me_y) & 1
    places = (tile >> 6) * RT + y * (RT // 2) + x * PT + (tile & 7)
    live = iota((1, TPD), 1) < count[0, 0]
    at_col = indicator((iota((CT, TPD), 0) == places) & live)
    copies[3].wait()
    for group in range(VEC // GROUP):
        for half in range(TPD // LANES):
            lanes = pl.ds(half * LANES, LANES)

            def step(a, totals):
                tile = tiles[a, :, lanes]
                return tuple(
                    total + tile * picked[half, pl.ds((group * GROUP + v) * TILE + a, 1), :]
                    for v, total in enumerate(totals)
                )

            zero = jnp.zeros((TILE, LANES), jnp.float32)
            totals = lax.fori_loop(0, TILE, step, (zero,) * GROUP, unroll=64)
            for v, total in enumerate(totals):
                summed[half, v * TILE : (v + 1) * TILE, :] = total
        out[:, group * GROUP * TILE : (group + 1) * GROUP * TILE] = place(at_col, whole(summed))
    for copy in copies[4:]:
        copy.wait()


def forward_kernel(count, row, *refs):
    chunks, refs = refs[:CHUNKS], refs[CHUNKS:]
    cids_far, rids_far, far, out, cids, rids, tiles, arrived, picked, summed = refs
    copies = fetch([(cids_far, cids), (rids_far, rids), (far, tiles)], arrived)
    for copy in copies[:2]:
        copy.wait()
    tile = cids[...]
    x, rest = (tile >> 4) & 3, (tile >> 6) * (NY * PT) + (tile & 15)
    places = (((row[0, 0] >> 1) - x) & 3) * CHUNK + rest
    side = jnp.concatenate([chunk[...] for chunk in chunks])
    pick(picked, indicator(iota((CT, TPD), 0) == places), side)
    live = iota((1, TPD), 1) < count[0, 0]
    at_row = indicator((iota((RT, TPD), 0) == rids[...]) & live)
    copies[2].wait()
    for group in range(VEC // GROUP):
        for half in range(TPD // LANES):
            lanes = pl.ds(half * LANES, LANES)
            blocks = [
                picked[half, (group * GROUP + v) * TILE : (group * GROUP + v + 1) * TILE, :]
                for v in range(GROUP)
            ]

            def step(a, carry):
                tile = tiles[a, :, lanes]
                for v, block in enumerate(blocks):
                    summed[half, pl.ds(v * TILE + a, 1), :] = jnp.sum(
                        tile * block, axis=0, keepdims=True
                    )
                return carry

            lax.fori_loop(0, TILE, step, 0, unroll=64)
        out[:, group * GROUP * TILE : (group + 1) * GROUP * TILE] = place(at_row, whole(summed))


def run(kernel, outs, vmem_mib, scratch, scalars, near, far):
    in_vmem, in_hbm = (pl.BlockSpec(memory_space=space) for space in (pltpu.VMEM, pltpu.HBM))
    return pl.pallas_call(
        kernel,
        out_shape=[jax.ShapeDtypeStruct((rows, WIDE), jnp.float32) for rows in outs],
        in_specs=[pl.BlockSpec(memory_space=pltpu.SMEM)] * len(scalars)
        + [in_vmem] * len(near)
        + [in_hbm] * len(far),
        out_specs=[in_vmem] + [in_hbm] * (len(outs) - 1),
        scratch_shapes=scratch
        + [
            pltpu.VMEM((1, TPD), jnp.int32),
            pltpu.VMEM((1, TPD), jnp.int32),
            pltpu.VMEM((TILE, TILE, TPD), jnp.float32),
            pltpu.SemaphoreType.DMA((6,)),
            pltpu.VMEM((TPD // LANES, WIDE, LANES), jnp.float32),
            pltpu.VMEM((TPD // LANES, GROUP * TILE, LANES), jnp.float32),
        ],
        compiler_params=pltpu.CompilerParams(vmem_limit_bytes=vmem_mib * 1024 * 1024),
        cost_estimate=pl.CostEstimate(
            flops=10_000_000_000, bytes_accessed=8 * 1024 * 1024, transcendentals=0
        ),
    )(*scalars, *near, *far)


def local(vectors, tiles, tile_rows, tile_cols, tile_count):
    me, me_col = lax.axis_index("row"), lax.axis_index("col")
    piece = vectors.T.reshape(VEC, PT, TILE).transpose(1, 0, 2).reshape(PT, WIDE)
    block = tiles[0, 0].transpose(1, 2, 0)
    rids, cids = tile_rows[0], tile_cols[0]

    rows = lax.all_gather(
        piece, ("row", "col"), axis_index_groups=RING_GROUPS, axis=0, tiled=True
    )
    col_part, pair = run(
        backward_kernel,
        [CT, NY * PT],
        BACK_MIB,
        [pltpu.VMEM((RT, WIDE), jnp.float32)],
        (tile_count, me.reshape(1, 1), me_col.reshape(1, 1)),
        (),
        (rows, rids, cids, block),
    )
    col_sum = lax.psum_scatter(
        col_part, "row", axis_index_groups=Z_GROUPS, scatter_dimension=0, tiled=True
    )

    mine = lax.all_gather(
        pair,
        "row",
        axis_index_groups=Z_GROUPS,
        axis=0,
        tiled=True,
    )
    first, second = mine[: CHUNK // 2], mine[CHUNK // 2 :]
    left_first = lax.ppermute(first, "row", row_shift(dx=1))
    right_second = lax.ppermute(second, "row", row_shift(dx=-1))
    left_second = lax.ppermute(second, "row", row_shift(dx=1))
    right_first = lax.ppermute(first, "row", row_shift(dx=-1))
    far_first = lax.ppermute(left_first, "row", row_shift(dx=1))
    far_second = lax.ppermute(right_second, "row", row_shift(dx=-1))
    chunks = [mine, left_first, left_second, far_first, far_second, right_first, right_second]
    me_too, col_sum = lax.optimization_barrier((me.reshape(1, 1), col_sum))
    half = RT // 2
    from_y = lax.ppermute(col_sum[half:], "row", row_shift(dy=1))
    (row_part,) = run(
        forward_kernel, [RT], FORTH_MIB, [], (tile_count, me_too), chunks, (cids, rids, block)
    )
    row_terms = lax.all_to_all(row_part, "col", 0, 0, tiled=True).reshape(-1, PT, WIDE)
    col_terms = (col_sum[:half] + from_y).reshape(NX, PT, WIDE)
    total = col_terms[0]
    for d in range(1, NX):
        total = total + lax.ppermute(col_terms[d], "row", row_shift(dx=d))
    total = total + row_terms.sum(axis=0)
    return total.reshape(PT, VEC, TILE).transpose(1, 0, 2).reshape(VEC, S).T


def solution(mesh):
    placed = (
        P(("row", "col"), None),
        P("row", "col", None, None, None),
        P("row", "col", None),
        P("row", "col", None),
        P("row", "col"),
    )
    return jax.shard_map(
        local, mesh=mesh, in_specs=placed, out_specs=P(("row", "col"), None), check_vma=False
    )
```

```python
import jax
import jax.numpy as jnp
from jax import lax
from jax.experimental import pallas as pl
from jax.experimental.pallas import tpu as pltpu
from jax.sharding import PartitionSpec as P

VEC = 16
TILE = 64
TPD = 256
S = 512
RT = 64
CT = 768
NZ, NX, NY = 12, 4, 2
NCOL = 8
PT = S // TILE
WIDE = VEC * TILE
CHUNK = CT // NX
GROUP = 4
LANES = 128
CHUNKS = 7
BACK_MIB, FORTH_MIB = 58, 48


def row_index(z, x, y):
    return ((z % NZ) * NX + (x % NX)) * NY + (y % NY)


def row_shift(dx=0, dy=0):
    return [
        (row_index(z, x, y), row_index(z, x + dx, y + dy))
        for z in range(NZ)
        for x in range(NX)
        for y in range(NY)
    ]


Z_GROUPS = [[row_index(z, x, y) for z in range(NZ)] for x in range(NX) for y in range(NY)]
XY_GROUPS = [[row_index(z, x, y) for x in range(NX) for y in range(NY)] for z in range(NZ)]
RING_GROUPS = [
    [row_index(z, x, y) * NCOL + c for y in range(NY) for c in range(NCOL)]
    for z in range(NZ)
    for x in range(NX)
]


def three_parts(value):
    first = value.astype(jnp.bfloat16)
    rest = value - first.astype(jnp.float32)
    second = rest.astype(jnp.bfloat16)
    third = (rest - second.astype(jnp.float32)).astype(jnp.bfloat16)
    return first, second, third


def indicator(condition):
    return jnp.where(condition, 1.0, 0.0).astype(jnp.bfloat16)


def iota(shape, dim):
    return lax.broadcasted_iota(jnp.int32, shape, dim)


def put(halves, value):
    for half in range(TPD // LANES):
        halves[half] = value[:, half * LANES : (half + 1) * LANES]


def whole(halves):
    return jnp.concatenate([halves[half] for half in range(TPD // LANES)], axis=1)


def column(row):
    return jnp.broadcast_to(row, (8, row.shape[1])).T[:, :1]


def fetch(pairs, arrived):
    copies = [pltpu.make_async_copy(*pair, arrived.at[i]) for i, pair in enumerate(pairs)]
    for copy in copies:
        copy.start()
    return copies


def pick(picked, onehot, value):
    dims = (((0,), (0,)), ((), ()))
    put(
        picked,
        lax.dot_general(
            jnp.concatenate(three_parts(value)),
            jnp.concatenate([onehot] * 3),
            dims,
            preferred_element_type=jnp.float32,
        ),
    )


def place(onehot, value):
    return lax.dot_general(
        jnp.concatenate([onehot] * 3, axis=1),
        jnp.concatenate(three_parts(value), axis=1),
        (((1,), (1,)), ((), ())),
        preferred_element_type=jnp.float32,
    )


def backward_kernel(
    count, row, col, rows, rids_far, cids_far, far, out, pair, side, rids, cids, tiles, arrived, picked, summed
):
    own = rows.at[pl.ds(pl.multiple_of((row[0, 0] & 1) * RT, RT), RT)]
    pairs = [(own, side), (rids_far, rids), (cids_far, cids), (far, tiles)]
    for y in range(NY):
        piece = rows.at[pl.ds(pl.multiple_of(y * RT + col[0, 0] * PT, PT), PT)]
        pairs.append((piece, pair.at[pl.ds(y * PT, PT)]))
    copies = fetch(pairs, arrived)
    for copy in copies[:3]:
        copy.wait()
    pick(picked, indicator(iota((RT, TPD), 0) == rids[...]), side[...])
    live = iota((1, TPD), 1) < count[0, 0]
    at_col = indicator((iota((CT, TPD), 0) == cids[...]) & live)
    copies[3].wait()
    for group in range(VEC // GROUP):
        for half in range(TPD // LANES):
            lanes = pl.ds(half * LANES, LANES)

            def step(a, totals):
                tile = tiles[a, :, lanes]
                return tuple(
                    total + tile * picked[half, pl.ds((group * GROUP + v) * TILE + a, 1), :]
                    for v, total in enumerate(totals)
                )

            zero = jnp.zeros((TILE, LANES), jnp.float32)
            totals = lax.fori_loop(0, TILE, step, (zero,) * GROUP, unroll=64)
            for v, total in enumerate(totals):
                summed[half, v * TILE : (v + 1) * TILE, :] = total
        out[:, group * GROUP * TILE : (group + 1) * GROUP * TILE] = place(at_col, whole(summed))
    for copy in copies[4:]:
        copy.wait()


def forward_kernel(count, row, *refs):
    chunks, refs = refs[:CHUNKS], refs[CHUNKS:]
    cids_far, rids_far, far, out, cids, rids, tiles, arrived, picked, summed = refs
    copies = fetch([(cids_far, cids), (rids_far, rids), (far, tiles)], arrived)
    for copy in copies[:2]:
        copy.wait()
    tile = cids[...]
    x, rest = (tile >> 4) & 3, (tile >> 6) * (NY * PT) + (tile & 15)
    places = (((row[0, 0] >> 1) - x) & 3) * CHUNK + rest
    side = jnp.concatenate([chunk[...] for chunk in chunks])
    pick(picked, indicator(iota((CT, TPD), 0) == places), side)
    live = iota((1, TPD), 1) < count[0, 0]
    at_row = indicator((iota((RT, TPD), 0) == rids[...]) & live)
    copies[2].wait()
    for group in range(VEC // GROUP):
        for half in range(TPD // LANES):
            lanes = pl.ds(half * LANES, LANES)
            blocks = [
                picked[half, (group * GROUP + v) * TILE : (group * GROUP + v + 1) * TILE, :]
                for v in range(GROUP)
            ]

            def step(a, carry):
                tile = tiles[a, :, lanes]
                for v, block in enumerate(blocks):
                    summed[half, pl.ds(v * TILE + a, 1), :] = jnp.sum(
                        tile * block, axis=0, keepdims=True
                    )
                return carry

            lax.fori_loop(0, TILE, step, 0, unroll=64)
        out[:, group * GROUP * TILE : (group + 1) * GROUP * TILE] = place(at_row, whole(summed))


def run(kernel, outs, vmem_mib, scratch, scalars, near, far):
    in_vmem, in_hbm = (pl.BlockSpec(memory_space=space) for space in (pltpu.VMEM, pltpu.HBM))
    return pl.pallas_call(
        kernel,
        out_shape=[jax.ShapeDtypeStruct((rows, WIDE), jnp.float32) for rows in outs],
        in_specs=[pl.BlockSpec(memory_space=pltpu.SMEM)] * len(scalars)
        + [in_vmem] * len(near)
        + [in_hbm] * len(far),
        out_specs=[in_vmem] + [in_hbm] * (len(outs) - 1),
        scratch_shapes=scratch
        + [
            pltpu.VMEM((1, TPD), jnp.int32),
            pltpu.VMEM((1, TPD), jnp.int32),
            pltpu.VMEM((TILE, TILE, TPD), jnp.float32),
            pltpu.SemaphoreType.DMA((6,)),
            pltpu.VMEM((TPD // LANES, WIDE, LANES), jnp.float32),
            pltpu.VMEM((TPD // LANES, GROUP * TILE, LANES), jnp.float32),
        ],
        compiler_params=pltpu.CompilerParams(vmem_limit_bytes=vmem_mib * 1024 * 1024),
        cost_estimate=pl.CostEstimate(
            flops=10_000_000_000, bytes_accessed=8 * 1024 * 1024, transcendentals=0
        ),
    )(*scalars, *near, *far)


def local(vectors, tiles, tile_rows, tile_cols, tile_count):
    me, me_col = lax.axis_index("row"), lax.axis_index("col")
    piece = vectors.T.reshape(VEC, PT, TILE).transpose(1, 0, 2).reshape(PT, WIDE)
    block = tiles[0, 0].transpose(1, 2, 0)
    rids, cids = tile_rows[0], tile_cols[0]

    rows = lax.all_gather(
        piece, ("row", "col"), axis_index_groups=RING_GROUPS, axis=0, tiled=True
    )
    col_part, pair = run(
        backward_kernel,
        [CT, NY * PT],
        BACK_MIB,
        [pltpu.VMEM((RT, WIDE), jnp.float32)],
        (tile_count, me.reshape(1, 1), me_col.reshape(1, 1)),
        (),
        (rows, rids, cids, block),
    )
    col_sum = lax.psum_scatter(
        col_part, "row", axis_index_groups=Z_GROUPS, scatter_dimension=0, tiled=True
    )

    mine = lax.all_gather(
        pair,
        "row",
        axis_index_groups=Z_GROUPS,
        axis=0,
        tiled=True,
    )
    first, second = mine[: CHUNK // 2], mine[CHUNK // 2 :]
    left_first = lax.ppermute(first, "row", row_shift(dx=1))
    right_second = lax.ppermute(second, "row", row_shift(dx=-1))
    left_second = lax.ppermute(second, "row", row_shift(dx=1))
    right_first = lax.ppermute(first, "row", row_shift(dx=-1))
    far_first = lax.ppermute(left_first, "row", row_shift(dx=1))
    far_second = lax.ppermute(right_second, "row", row_shift(dx=-1))
    chunks = [mine, left_first, left_second, far_first, far_second, right_first, right_second]
    me_too, col_sum = lax.optimization_barrier((me.reshape(1, 1), col_sum))
    col_terms = lax.all_to_all(
        col_sum, "row", 0, 0, axis_index_groups=XY_GROUPS, tiled=True
    ).reshape(NX * NY, PT, WIDE)
    (row_part,) = run(
        forward_kernel, [RT], FORTH_MIB, [], (tile_count, me_too), chunks, (cids, rids, block)
    )
    row_terms = lax.all_to_all(row_part, "col", 0, 0, tiled=True).reshape(-1, PT, WIDE)
    total = col_terms.sum(axis=0) + row_terms.sum(axis=0)
    return total.reshape(PT, VEC, TILE).transpose(1, 0, 2).reshape(VEC, S).T


def solution(mesh):
    placed = (
        P(("row", "col"), None),
        P("row", "col", None, None, None),
        P("row", "col", None),
        P("row", "col", None),
        P("row", "col"),
    )
    return jax.shard_map(
        local, mesh=mesh, in_specs=placed, out_specs=P(("row", "col"), None), check_vma=False
    )
```

```python
import jax
import jax.numpy as jnp
from jax import lax
from jax.experimental import pallas as pl
from jax.experimental.pallas import tpu as pltpu
from jax.sharding import PartitionSpec as P

VEC = 16
TILE = 64
TPD = 256
S = 512
RT = 64
CT = 768
NZ, NX, NY = 12, 4, 2
NCOL, NYL = 8, 4
PT = S // TILE
WIDE = VEC * TILE
CHUNK = CT // NX
GROUP = 4
LANES = 128
CHUNKS = 7
BACK_MIB, FORTH_MIB = 58, 48


def row_index(z, x, y):
    return ((z % NZ) * NX + (x % NX)) * NY + (y % NY)


def col_shift(dy=0, core=0):
    return [
        (y * 2 + k, ((y + dy) % NYL) * 2 + (k ^ core)) for y in range(NYL) for k in range(2)
    ]


def row_shift(dx=0, dy=0):
    return [
        (row_index(z, x, y), row_index(z, x + dx, y + dy))
        for z in range(NZ)
        for x in range(NX)
        for y in range(NY)
    ]


Z_GROUPS = [[row_index(z, x, y) for z in range(NZ)] for x in range(NX) for y in range(NY)]
XY_GROUPS = [[row_index(z, x, y) for x in range(NX) for y in range(NY)] for z in range(NZ)]
RING_GROUPS = [
    [row_index(z, x, y) * NCOL + c for y in range(NY) for c in range(NCOL)]
    for z in range(NZ)
    for x in range(NX)
]


def three_parts(value):
    first = value.astype(jnp.bfloat16)
    rest = value - first.astype(jnp.float32)
    second = rest.astype(jnp.bfloat16)
    third = (rest - second.astype(jnp.float32)).astype(jnp.bfloat16)
    return first, second, third


def indicator(condition):
    return jnp.where(condition, 1.0, 0.0).astype(jnp.bfloat16)


def iota(shape, dim):
    return lax.broadcasted_iota(jnp.int32, shape, dim)


def put(halves, value):
    for half in range(TPD // LANES):
        halves[half] = value[:, half * LANES : (half + 1) * LANES]


def whole(halves):
    return jnp.concatenate([halves[half] for half in range(TPD // LANES)], axis=1)


def column(row):
    return jnp.broadcast_to(row, (8, row.shape[1])).T[:, :1]


def fetch(pairs, arrived):
    copies = [pltpu.make_async_copy(*pair, arrived.at[i]) for i, pair in enumerate(pairs)]
    for copy in copies:
        copy.start()
    return copies


def pick(picked, onehot, value):
    dims = (((0,), (0,)), ((), ()))
    put(
        picked,
        lax.dot_general(
            jnp.concatenate(three_parts(value)),
            jnp.concatenate([onehot] * 3),
            dims,
            preferred_element_type=jnp.float32,
        ),
    )


def place(onehot, value):
    return lax.dot_general(
        jnp.concatenate([onehot] * 3, axis=1),
        jnp.concatenate(three_parts(value), axis=1),
        (((1,), (1,)), ((), ())),
        preferred_element_type=jnp.float32,
    )


def backward_kernel(
    count, row, col, rows, rids_far, cids_far, far, out, pair, side, rids, cids, tiles, arrived, picked, summed
):
    own = rows.at[pl.ds(pl.multiple_of((row[0, 0] & 1) * RT, RT), RT)]
    pairs = [(own, side), (rids_far, rids), (cids_far, cids), (far, tiles)]
    for y in range(NY):
        piece = rows.at[pl.ds(pl.multiple_of(y * RT + col[0, 0] * PT, PT), PT)]
        pairs.append((piece, pair.at[pl.ds(y * PT, PT)]))
    copies = fetch(pairs, arrived)
    for copy in copies[:3]:
        copy.wait()
    pick(picked, indicator(iota((RT, TPD), 0) == rids[...]), side[...])
    live = iota((1, TPD), 1) < count[0, 0]
    at_col = indicator((iota((CT, TPD), 0) == cids[...]) & live)
    copies[3].wait()
    for group in range(VEC // GROUP):
        for half in range(TPD // LANES):
            lanes = pl.ds(half * LANES, LANES)

            def step(a, totals):
                tile = tiles[a, :, lanes]
                return tuple(
                    total + tile * picked[half, pl.ds((group * GROUP + v) * TILE + a, 1), :]
                    for v, total in enumerate(totals)
                )

            zero = jnp.zeros((TILE, LANES), jnp.float32)
            totals = lax.fori_loop(0, TILE, step, (zero,) * GROUP, unroll=64)
            for v, total in enumerate(totals):
                summed[half, v * TILE : (v + 1) * TILE, :] = total
        out[:, group * GROUP * TILE : (group + 1) * GROUP * TILE] = place(at_col, whole(summed))
    for copy in copies[4:]:
        copy.wait()


def forward_kernel(count, row, col, *refs):
    chunks, refs = refs[:CHUNKS], refs[CHUNKS:]
    cids_far, rids_far, far, own, mate, cids, rids, tiles, arrived, picked, summed = refs
    copies = fetch([(cids_far, cids), (rids_far, rids), (far, tiles)], arrived)
    for copy in copies[:2]:
        copy.wait()
    tile = cids[...]
    x, rest = (tile >> 4) & 3, (tile >> 6) * (NY * PT) + (tile & 15)
    places = (((row[0, 0] >> 1) - x) & 3) * CHUNK + rest
    side = jnp.concatenate([chunk[...] for chunk in chunks])
    pick(picked, indicator(iota((CT, TPD), 0) == places), side)
    live = iota((1, TPD), 1) < count[0, 0]
    tile, me = rids[...], col[0, 0]
    core, y = ((tile >> 3) ^ me) & 1, ((tile >> 4) - (me >> 1)) & 3
    places = core * (RT // 2) + y * PT + (tile & 7)
    at_row = indicator((iota((RT, TPD), 0) == places) & live)
    copies[2].wait()
    for group in range(VEC // GROUP):
        for half in range(TPD // LANES):
            lanes = pl.ds(half * LANES, LANES)
            blocks = [
                picked[half, (group * GROUP + v) * TILE : (group * GROUP + v + 1) * TILE, :]
                for v in range(GROUP)
            ]

            def step(a, carry):
                tile = tiles[a, :, lanes]
                for v, block in enumerate(blocks):
                    summed[half, pl.ds(v * TILE + a, 1), :] = jnp.sum(
                        tile * block, axis=0, keepdims=True
                    )
                return carry

            lax.fori_loop(0, TILE, step, 0, unroll=64)
        columns = slice(group * GROUP * TILE, (group + 1) * GROUP * TILE)
        sums = place(at_row, whole(summed))
        own[:, columns], mate[:, columns] = sums[: RT // 2], sums[RT // 2 :]


def run(kernel, outs, vmem_mib, scratch, scalars, near, far):
    in_vmem, in_hbm = (pl.BlockSpec(memory_space=space) for space in (pltpu.VMEM, pltpu.HBM))
    return pl.pallas_call(
        kernel,
        out_shape=[jax.ShapeDtypeStruct((rows, WIDE), jnp.float32) for rows in outs],
        in_specs=[pl.BlockSpec(memory_space=pltpu.SMEM)] * len(scalars)
        + [in_vmem] * len(near)
        + [in_hbm] * len(far),
        out_specs=[in_vmem] + [in_hbm if scratch else in_vmem] * (len(outs) - 1),
        scratch_shapes=scratch
        + [
            pltpu.VMEM((1, TPD), jnp.int32),
            pltpu.VMEM((1, TPD), jnp.int32),
            pltpu.VMEM((TILE, TILE, TPD), jnp.float32),
            pltpu.SemaphoreType.DMA((6,)),
            pltpu.VMEM((TPD // LANES, WIDE, LANES), jnp.float32),
            pltpu.VMEM((TPD // LANES, GROUP * TILE, LANES), jnp.float32),
        ],
        compiler_params=pltpu.CompilerParams(vmem_limit_bytes=vmem_mib * 1024 * 1024),
        cost_estimate=pl.CostEstimate(
            flops=10_000_000_000, bytes_accessed=8 * 1024 * 1024, transcendentals=0
        ),
    )(*scalars, *near, *far)


def local(vectors, tiles, tile_rows, tile_cols, tile_count):
    me, me_col = lax.axis_index("row"), lax.axis_index("col")
    piece = vectors.T.reshape(VEC, PT, TILE).transpose(1, 0, 2).reshape(PT, WIDE)
    block = tiles[0, 0].transpose(1, 2, 0)
    rids, cids = tile_rows[0], tile_cols[0]

    rows = lax.all_gather(
        piece, ("row", "col"), axis_index_groups=RING_GROUPS, axis=0, tiled=True
    )
    col_part, pair = run(
        backward_kernel,
        [CT, NY * PT],
        BACK_MIB,
        [pltpu.VMEM((RT, WIDE), jnp.float32)],
        (tile_count, me.reshape(1, 1), me_col.reshape(1, 1)),
        (),
        (rows, rids, cids, block),
    )
    col_sum = lax.psum_scatter(
        col_part, "row", axis_index_groups=Z_GROUPS, scatter_dimension=0, tiled=True
    )

    mine = lax.all_gather(
        pair,
        "row",
        axis_index_groups=Z_GROUPS,
        axis=0,
        tiled=True,
    )
    first, second = mine[: CHUNK // 2], mine[CHUNK // 2 :]
    left_first = lax.ppermute(first, "row", row_shift(dx=1))
    right_second = lax.ppermute(second, "row", row_shift(dx=-1))
    left_second = lax.ppermute(second, "row", row_shift(dx=1))
    right_first = lax.ppermute(first, "row", row_shift(dx=-1))
    far_first = lax.ppermute(left_first, "row", row_shift(dx=1))
    far_second = lax.ppermute(right_second, "row", row_shift(dx=-1))
    chunks = [mine, left_first, left_second, far_first, far_second, right_first, right_second]
    own, others = run(
        forward_kernel,
        [RT // 2, RT // 2],
        FORTH_MIB,
        [],
        (tile_count, me.reshape(1, 1), me_col.reshape(1, 1)),
        chunks,
        (cids, rids, block),
    )
    own, col_sum = lax.optimization_barrier((own, col_sum))
    col_terms = lax.all_to_all(
        col_sum, "row", 0, 0, axis_index_groups=XY_GROUPS, tiled=True
    ).reshape(NX * NY, PT, WIDE)
    mate = lax.ppermute(others, "col", col_shift(core=1))
    halves = (own + mate).reshape(NYL, PT, WIDE)
    row_total = halves[0]
    for d in range(1, NYL):
        row_total = row_total + lax.ppermute(halves[d], "col", col_shift(dy=d))
    total = col_terms.sum(axis=0) + row_total
    return total.reshape(PT, VEC, TILE).transpose(1, 0, 2).reshape(VEC, S).T


def solution(mesh):
    placed = (
        P(("row", "col"), None),
        P("row", "col", None, None, None),
        P("row", "col", None),
        P("row", "col", None),
        P("row", "col"),
    )
    return jax.shard_map(
        local, mesh=mesh, in_specs=placed, out_specs=P(("row", "col"), None), check_vma=False
    )
```

```python
import jax
import jax.numpy as jnp
from jax import lax
from jax.experimental import pallas as pl
from jax.experimental.pallas import tpu as pltpu
from jax.sharding import PartitionSpec as P

VEC = 16
TILE = 64
TPD = 256
S = 512
RT = 64
CT = 768
NZ, NX, NY = 12, 4, 2
NCOL, NYL = 8, 4
PT = S // TILE
WIDE = VEC * TILE
CHUNK = CT // NX
GROUP = 4
LANES = 128
BACK_MIB, FORTH_MIB = 58, 48


def row_index(z, x, y):
    return ((z % NZ) * NX + (x % NX)) * NY + (y % NY)


def col_shift(dy=0, core=0):
    return [
        (y * 2 + k, ((y + dy) % NYL) * 2 + (k ^ core)) for y in range(NYL) for k in range(2)
    ]


def row_shift(dx=0, dy=0):
    return [
        (row_index(z, x, y), row_index(z, x + dx, y + dy))
        for z in range(NZ)
        for x in range(NX)
        for y in range(NY)
    ]


Z_GROUPS = [[row_index(z, x, y) for z in range(NZ)] for x in range(NX) for y in range(NY)]
XY_GROUPS = [[row_index(z, x, y) for x in range(NX) for y in range(NY)] for z in range(NZ)]
RING_GROUPS = [
    [row_index(z, x, y) * NCOL + c for y in range(NY) for c in range(NCOL)]
    for z in range(NZ)
    for x in range(NX)
]


def three_parts(value):
    first = value.astype(jnp.bfloat16)
    rest = value - first.astype(jnp.float32)
    second = rest.astype(jnp.bfloat16)
    third = (rest - second.astype(jnp.float32)).astype(jnp.bfloat16)
    return first, second, third


def indicator(condition):
    return jnp.where(condition, 1.0, 0.0).astype(jnp.bfloat16)


def iota(shape, dim):
    return lax.broadcasted_iota(jnp.int32, shape, dim)


def put(halves, value):
    for half in range(TPD // LANES):
        halves[half] = value[:, half * LANES : (half + 1) * LANES]


def whole(halves):
    return jnp.concatenate([halves[half] for half in range(TPD // LANES)], axis=1)


def column(row):
    return jnp.broadcast_to(row, (8, row.shape[1])).T[:, :1]


def fetch(pairs, arrived):
    copies = [pltpu.make_async_copy(*pair, arrived.at[i]) for i, pair in enumerate(pairs)]
    for copy in copies:
        copy.start()
    return copies


def pick(picked, onehot, value, before=None):
    found = lax.dot_general(
        jnp.concatenate(three_parts(value)),
        jnp.concatenate([onehot] * 3),
        (((0,), (0,)), ((), ())),
        preferred_element_type=jnp.float32,
    )
    put(picked, found if before is None else found + whole(before))


def place(onehot, value):
    return lax.dot_general(
        jnp.concatenate([onehot] * 3, axis=1),
        jnp.concatenate(three_parts(value), axis=1),
        (((1,), (1,)), ((), ())),
        preferred_element_type=jnp.float32,
    )


def backward_kernel(
    count, row, col, rows, rids_far, cids_far, far, out, pair, side, rids, cids, tiles, arrived, picked, summed
):
    own = rows.at[pl.ds(pl.multiple_of((row[0, 0] & 1) * RT, RT), RT)]
    pairs = [(own, side), (rids_far, rids), (cids_far, cids), (far, tiles)]
    for y in range(NY):
        piece = rows.at[pl.ds(pl.multiple_of(y * RT + col[0, 0] * PT, PT), PT)]
        pairs.append((piece, pair.at[pl.ds(y * PT, PT)]))
    copies = fetch(pairs, arrived)
    for copy in copies[:3]:
        copy.wait()
    pick(picked, indicator(iota((RT, TPD), 0) == rids[...]), side[...])
    live = iota((1, TPD), 1) < count[0, 0]
    at_col = indicator((iota((CT, TPD), 0) == cids[...]) & live)
    copies[3].wait()
    for group in range(VEC // GROUP):
        for half in range(TPD // LANES):
            lanes = pl.ds(half * LANES, LANES)

            def step(a, totals):
                tile = tiles[a, :, lanes]
                return tuple(
                    total + tile * picked[half, pl.ds((group * GROUP + v) * TILE + a, 1), :]
                    for v, total in enumerate(totals)
                )

            zero = jnp.zeros((TILE, LANES), jnp.float32)
            totals = lax.fori_loop(0, TILE, step, (zero,) * GROUP, unroll=64)
            for v, total in enumerate(totals):
                summed[half, v * TILE : (v + 1) * TILE, :] = total
        out[:, group * GROUP * TILE : (group + 1) * GROUP * TILE] = place(at_col, whole(summed))
    for copy in copies[4:]:
        copy.wait()


def places_of(tile, row):
    x, rest = (tile >> 4) & 3, (tile >> 6) * (NY * PT) + (tile & 15)
    return (((row >> 1) - x) & 3) * CHUNK + rest


def near_kernel(row, *refs):
    chunks, (cids, found) = refs[:-2], refs[-2:]
    places = places_of(cids[...], row[0, 0])
    places = jnp.where(places < 2 * CHUNK, places, jnp.where(places < 3 * CHUNK, -1, places - CHUNK))
    side = jnp.concatenate([chunk[...] for chunk in chunks])
    pick(found, indicator(iota((3 * CHUNK, TPD), 0) == places), side)


def forward_kernel(count, row, col, *refs):
    found, far_first, far_second, refs = *refs[:3], refs[3:]
    cids_far, rids_far, far, own, mate, cids, rids, tiles, arrived, picked, summed = refs
    copies = fetch([(cids_far, cids), (rids_far, rids), (far, tiles)], arrived)
    for copy in copies[:2]:
        copy.wait()
    places = places_of(cids[...], row[0, 0]) - 2 * CHUNK
    side = jnp.concatenate([far_first[...], far_second[...]])
    pick(picked, indicator(iota((CHUNK, TPD), 0) == places), side, found)
    live = iota((1, TPD), 1) < count[0, 0]
    tile, me = rids[...], col[0, 0]
    core, y = ((tile >> 3) ^ me) & 1, ((tile >> 4) - (me >> 1)) & 3
    places = core * (RT // 2) + y * PT + (tile & 7)
    at_row = indicator((iota((RT, TPD), 0) == places) & live)
    copies[2].wait()
    for group in range(VEC // GROUP):
        for half in range(TPD // LANES):
            lanes = pl.ds(half * LANES, LANES)
            blocks = [
                picked[half, (group * GROUP + v) * TILE : (group * GROUP + v + 1) * TILE, :]
                for v in range(GROUP)
            ]

            def step(a, carry):
                tile = tiles[a, :, lanes]
                for v, block in enumerate(blocks):
                    summed[half, pl.ds(v * TILE + a, 1), :] = jnp.sum(
                        tile * block, axis=0, keepdims=True
                    )
                return carry

            lax.fori_loop(0, TILE, step, 0, unroll=64)
        columns = slice(group * GROUP * TILE, (group + 1) * GROUP * TILE)
        sums = place(at_row, whole(summed))
        own[:, columns], mate[:, columns] = sums[: RT // 2], sums[RT // 2 :]


def run(kernel, outs, vmem_mib, scratch, scalars, near, far):
    in_vmem, in_hbm = (pl.BlockSpec(memory_space=space) for space in (pltpu.VMEM, pltpu.HBM))
    return pl.pallas_call(
        kernel,
        out_shape=[jax.ShapeDtypeStruct((rows, WIDE), jnp.float32) for rows in outs],
        in_specs=[pl.BlockSpec(memory_space=pltpu.SMEM)] * len(scalars)
        + [in_vmem] * len(near)
        + [in_hbm] * len(far),
        out_specs=[in_vmem] + [in_hbm if scratch else in_vmem] * (len(outs) - 1),
        scratch_shapes=scratch
        + [
            pltpu.VMEM((1, TPD), jnp.int32),
            pltpu.VMEM((1, TPD), jnp.int32),
            pltpu.VMEM((TILE, TILE, TPD), jnp.float32),
            pltpu.SemaphoreType.DMA((6,)),
            pltpu.VMEM((TPD // LANES, WIDE, LANES), jnp.float32),
            pltpu.VMEM((TPD // LANES, GROUP * TILE, LANES), jnp.float32),
        ],
        compiler_params=pltpu.CompilerParams(vmem_limit_bytes=vmem_mib * 1024 * 1024),
        cost_estimate=pl.CostEstimate(
            flops=10_000_000_000, bytes_accessed=8 * 1024 * 1024, transcendentals=0
        ),
    )(*scalars, *near, *far)


def local(vectors, tiles, tile_rows, tile_cols, tile_count):
    me, me_col = lax.axis_index("row"), lax.axis_index("col")
    piece = vectors.T.reshape(VEC, PT, TILE).transpose(1, 0, 2).reshape(PT, WIDE)
    block = tiles[0, 0].transpose(1, 2, 0)
    rids, cids = tile_rows[0], tile_cols[0]

    rows = lax.all_gather(
        piece, ("row", "col"), axis_index_groups=RING_GROUPS, axis=0, tiled=True
    )
    col_part, pair = run(
        backward_kernel,
        [CT, NY * PT],
        BACK_MIB,
        [pltpu.VMEM((RT, WIDE), jnp.float32)],
        (tile_count, me.reshape(1, 1), me_col.reshape(1, 1)),
        (),
        (rows, rids, cids, block),
    )
    col_sum = lax.psum_scatter(
        col_part, "row", axis_index_groups=Z_GROUPS, scatter_dimension=0, tiled=True
    )

    mine = lax.all_gather(
        pair,
        "row",
        axis_index_groups=Z_GROUPS,
        axis=0,
        tiled=True,
    )
    first, second = mine[: CHUNK // 2], mine[CHUNK // 2 :]
    left_first = lax.ppermute(first, "row", row_shift(dx=1))
    right_second = lax.ppermute(second, "row", row_shift(dx=-1))
    left_second = lax.ppermute(second, "row", row_shift(dx=1))
    right_first = lax.ppermute(first, "row", row_shift(dx=-1))
    far_first = lax.ppermute(left_first, "row", row_shift(dx=1))
    far_second = lax.ppermute(right_second, "row", row_shift(dx=-1))
    in_vmem = pl.BlockSpec(memory_space=pltpu.VMEM)
    found = pl.pallas_call(
        near_kernel,
        out_shape=jax.ShapeDtypeStruct((TPD // LANES, WIDE, LANES), jnp.float32),
        in_specs=[pl.BlockSpec(memory_space=pltpu.SMEM)] + [in_vmem] * 6,
        out_specs=in_vmem,
        compiler_params=pltpu.CompilerParams(vmem_limit_bytes=FORTH_MIB * 1024 * 1024),
    )(me.reshape(1, 1), mine, left_first, left_second, right_first, right_second, cids)
    own, others = run(
        forward_kernel,
        [RT // 2, RT // 2],
        FORTH_MIB,
        [],
        (tile_count, me.reshape(1, 1), me_col.reshape(1, 1)),
        (found, far_first, far_second),
        (cids, rids, block),
    )
    own, col_sum = lax.optimization_barrier((own, col_sum))
    col_terms = lax.all_to_all(
        col_sum, "row", 0, 0, axis_index_groups=XY_GROUPS, tiled=True
    ).reshape(NX * NY, PT, WIDE)
    mate = lax.ppermute(others, "col", col_shift(core=1))
    halves = (own + mate).reshape(NYL, PT, WIDE)
    row_total = halves[0]
    for d in range(1, NYL):
        row_total = row_total + lax.ppermute(halves[d], "col", col_shift(dy=d))
    total = col_terms.sum(axis=0) + row_total
    return total.reshape(PT, VEC, TILE).transpose(1, 0, 2).reshape(VEC, S).T


def solution(mesh):
    placed = (
        P(("row", "col"), None),
        P("row", "col", None, None, None),
        P("row", "col", None),
        P("row", "col", None),
        P("row", "col"),
    )
    return jax.shard_map(
        local, mesh=mesh, in_specs=placed, out_specs=P(("row", "col"), None), check_vma=False
    )
```
